32 devices in a mesh: seq: 8 (over z, x), head: 4 (over y, core).
Axes of the slice: x: 2, y: 2, z: 4, core: 2. Of those that a mesh axis runs over, the one named last changes fastest.
Arguments:
- grad_out: bfloat16 [1024, 3072], P('seq', 'head'), may hold values from -6 to 6
- out_weight: bfloat16 [3072, 3072], P('head', 'seq'), may hold values from -0.109375 to 0.109375
- row_owner: int32 [1024], P('seq'), may hold values from 0 to 7, as said below
- row_position: int32 [1024], P('seq'), may hold values from 0 to 127, as said below
- query_rows: bfloat16 [1024, 3072], P('seq', 'head'), may hold values from -48 to 48
- key_rows: bfloat16 [1024, 3072], P('seq', 'head'), may hold values from -48 to 48
- value_rows: bfloat16 [1024, 3072], P('seq', 'head'), may hold values from -6 to 6
- band_widths: int32 [8, 2], P('seq'), may hold values from 16 to 64, as said below
Outputs:
- grad_query: bfloat16 [1024, 3072], P('seq', 'head')
- grad_key: bfloat16 [1024, 3072], P('seq', 'head')
- grad_value: bfloat16 [1024, 3072], P('seq', 'head')
The draws below stay inside these ranges and needn't reach their ends.
Inputs may be any that keep to these rules, and one draw needn't show every extreme that they name: `row_owner`: each frame receives each of its 128 positions from exactly one packed row. One device holds at most 24 rows of one frame, and every device holds exactly 24 rows of some frame; how many rows device s holds of frame o depends only on (o - s) mod 8, and is at least one for (o - s) mod 8 equal to 1, 4 and 7. `row_position`: together with row_owner, a permutation of all tokens. `band_widths`: column 0 lies in 32 to 64, column 1 in 16 to 32.
All inputs are finite; a program needn't handle non-finite values.
Results may differ from the reference program's by a relative error of at most 0.0088.
Values may be sent and summed in bfloat16 or wider, within the bound.
A program may use at most 64 MiB of HBM per device.

```python
import jax
import jax.numpy as jnp
from jax import lax

D = 3072
HEADS = 24
HEAD_DIM = 128
FRAME_TOK = 128
FRAMES = 8
TOKENS = 1024
CAP = 24


def routing(key):
    folded = jax.random.fold_in(key, 11)
    key_vals, key_pick, key_slots, key_places = jax.random.split(folded, 4)
    ranking = jax.random.permutation(key_vals, FRAMES)
    ranking = ranking.at[FRAMES // 2].set(-3)
    ranking = ranking.at[1].set(-2)
    ranking = ranking.at[FRAMES - 1].set(-1)
    order_vals = jnp.argsort(ranking, stable=True)
    offsets_all = jnp.repeat(order_vals, CAP)
    remaining = jax.random.permutation(key_pick, FRAMES * CAP - 3 * CAP) + 3 * CAP
    chosen = jnp.concatenate([jnp.arange(CAP), jnp.array([CAP, 2 * CAP]), remaining[:FRAME_TOK - CAP - 2]])
    offsets = offsets_all[chosen]

    def shuffled(subkey):
        return jax.random.permutation(subkey, FRAME_TOK)
    slot_order = jax.vmap(shuffled)(jax.random.split(key_slots, FRAMES))
    places = jax.vmap(shuffled)(jax.random.split(key_places, FRAMES))
    device = jnp.arange(FRAMES)[:, None]
    owner = (device + offsets[slot_order]) % FRAMES
    position = places[owner, slot_order]
    return (owner.reshape(-1).astype(jnp.int32), position.reshape(-1).astype(jnp.int32))


def draw_row_owner(key, part):
    return routing(key)[0]


def draw_row_position(key, part):
    return routing(key)[1]


def draw_band_widths(key, part):
    folded = jax.random.fold_in(key, 23)
    key_half, key_quarter, key_frame = jax.random.split(folded, 3)
    half = jax.random.randint(key_half, (FRAMES,), FRAME_TOK // 4, FRAME_TOK // 2 + 1)
    quarter = jax.random.randint(key_quarter, (FRAMES,), FRAME_TOK // 8, FRAME_TOK // 4 + 1)
    chosen = jax.random.randint(key_frame, (), 0, FRAMES)
    marked = jnp.arange(FRAMES) == chosen
    half = jnp.where(marked, FRAME_TOK // 2, half)
    quarter = jnp.where(marked, FRAME_TOK // 8, quarter)
    return jnp.stack([half, quarter], axis=1).astype(jnp.int32)


def attention_pair(key):
    folded = jax.random.fold_in(key, 31)
    subkeys = jax.random.split(folded, 2)
    layout = (TOKENS, HEADS, HEAD_DIM)
    queries = jnp.clip(jax.random.normal(subkeys[0], layout, jnp.float32), -6.0, 6.0)
    keys_all = jnp.clip(jax.random.normal(subkeys[1], layout, jnp.float32), -6.0, 6.0)
    return (queries.reshape(TOKENS, D), keys_all.reshape(TOKENS, D))


def draw_query_rows(key, part):
    return attention_pair(key)[0].astype(jnp.bfloat16)


def draw_key_rows(key, part):
    return attention_pair(key)[1].astype(jnp.bfloat16)


def levels(own_key, shape, cuts, low, largest):
    gain = 1.0
    for dim, parts in cuts:
        steps = jax.random.uniform(jax.random.fold_in(jax.random.fold_in(own_key, 6), dim), (parts,), jnp.float32, low / len(cuts), largest / len(cuts))
        gain = gain * jnp.repeat(jnp.exp(steps), shape[dim] // parts).reshape((-1,) + (1,) * (len(shape) - 1 - dim))
    return gain


def centred(stream_key, shape, width, most, cuts=(), kind=jnp.bfloat16):
    result = jax.random.normal(stream_key, shape, jnp.float32) * width
    if len(cuts) > 0:
        result = levels(stream_key, shape, cuts, -0.22, 0.18) * result
    return jnp.clip(result, min=-most, max=most).astype(kind)


def setup_inputs(seed: int = 0) -> dict:
    key_list = jax.random.split(jax.random.key(seed), 9)
    return {
        "grad_out": centred(key_list[0], (TOKENS, D), 1.0, 6.0, ((0, 8), (1, 4))),
        "out_weight": centred(key_list[1], (D, D), D ** -0.5, 0.109375, ((0, 4), (1, 8))),
        "row_owner": draw_row_owner(jax.random.fold_in(key_list[8], 71), 0),
        "row_position": draw_row_position(jax.random.fold_in(key_list[8], 71), 0),
        "query_rows": draw_query_rows(jax.random.fold_in(key_list[8], 71), 0),
        "key_rows": draw_key_rows(jax.random.fold_in(key_list[8], 71), 0),
        "value_rows": centred(key_list[6], (TOKENS, D), 1.0, 6.0, ((0, 8), (1, 4))),
        "band_widths": draw_band_widths(jax.random.fold_in(key_list[8], 71), 0),
    }


DISTANCES = (0, 1, 2, 4)
NEG_FILL = -1.0e30


def reference(grad_out, out_weight, row_owner, row_position, query_rows, key_rows, value_rows, band_widths):
    packed = jnp.dot(grad_out, out_weight.T, preferred_element_type=jnp.float32).astype(jnp.bfloat16)
    target = (row_owner * FRAME_TOK + row_position).astype(jnp.int32)
    grad_attn = jnp.zeros_like(packed).at[target].set(packed)
    scale = HEAD_DIM ** -0.5
    margin = 4 * FRAME_TOK

    def padded(array):
        return jnp.pad(array, ((margin, margin), (0, 0)))

    query_pad = padded(query_rows)
    key_pad = padded(key_rows)
    value_pad = padded(value_rows)
    grad_pad = padded(grad_attn)
    positions = jnp.arange(FRAME_TOK, dtype=jnp.int32)
    spread = jnp.abs(positions[:, None] - positions[None, :])

    def frame_rows(array, frame):
        start = ((frame + 4) * FRAME_TOK).astype(jnp.int32)
        return lax.dynamic_slice_in_dim(array, start, FRAME_TOK, 0)

    def split_heads(array):
        return array.astype(jnp.float32).reshape(FRAME_TOK, HEADS, HEAD_DIM)

    def allowed(frame, distance):
        in_range = (frame - distance >= 0) & (frame < FRAMES)
        clipped = jnp.clip(frame, 0, FRAMES - 1)
        if distance == 2:
            limit = band_widths[clipped, 0]
        elif distance == 4:
            limit = band_widths[clipped, 1]
        else:
            limit = FRAME_TOK
        return (in_range & (spread < limit))[None]

    def logits(query_frame, key_frame):
        return jnp.einsum("ihc,jhc->hij", split_heads(query_frame), split_heads(key_frame)) * scale

    def to_half(array):
        return lax.optimization_barrier(array.astype(jnp.bfloat16)).astype(jnp.float32)

    def statistics(frame):
        queries = frame_rows(query_pad, frame)
        score_list = []
        mask_list = []
        value_list = []
        for distance in DISTANCES:
            score_list.append(logits(queries, frame_rows(key_pad, frame - distance)))
            mask_list.append(allowed(frame, distance))
            value_list.append(split_heads(frame_rows(value_pad, frame - distance)))
        scores = jnp.concatenate(score_list, axis=2)
        usable = jnp.concatenate(mask_list, axis=2)
        row_max = jnp.max(jnp.where(usable, scores, NEG_FILL), axis=2, keepdims=True)
        weights = jnp.where(usable, jnp.exp(scores - row_max), 0.0)
        row_sum = jnp.sum(weights, axis=2, keepdims=True)
        prob_half = to_half(weights / row_sum)
        values_all = jnp.concatenate(value_list, axis=0)
        attn_out = jnp.einsum("hij,jhc->ihc", prob_half, values_all)
        row_dot = jnp.sum(split_heads(frame_rows(grad_pad, frame)) * attn_out, axis=2).T
        return (row_max + jnp.log(row_sum))[:, :, 0], row_dot

    frames = jnp.arange(FRAMES, dtype=jnp.int32)
    log_norm, row_dots = lax.map(statistics, frames)

    def grad_queries(frame):
        queries = frame_rows(query_pad, frame)
        grads = split_heads(frame_rows(grad_pad, frame))
        norm_here = log_norm[frame][:, :, None]
        dot_here = row_dots[frame][:, :, None]
        total = jnp.zeros((FRAME_TOK, HEADS, HEAD_DIM), jnp.float32)
        for distance in DISTANCES:
            keys = frame_rows(key_pad, frame - distance)
            values = frame_rows(value_pad, frame - distance)
            prob = jnp.where(allowed(frame, distance), jnp.exp(logits(queries, keys) - norm_here), 0.0)
            grad_prob = jnp.einsum("ihc,jhc->hij", grads, split_heads(values))
            grad_score = to_half(prob * (grad_prob - dot_here))
            total = total + jnp.einsum("hij,jhc->ihc", grad_score, split_heads(keys))
        return (scale * total).reshape(FRAME_TOK, D).astype(jnp.bfloat16)

    def grad_keys(frame):
        keys = frame_rows(key_pad, frame)
        values = frame_rows(value_pad, frame)
        key_total = jnp.zeros((FRAME_TOK, HEADS, HEAD_DIM), jnp.float32)
        value_total = jnp.zeros((FRAME_TOK, HEADS, HEAD_DIM), jnp.float32)
        for distance in DISTANCES:
            source = frame + distance
            queries = frame_rows(query_pad, source)
            grads = split_heads(frame_rows(grad_pad, source))
            clipped = jnp.clip(source, 0, FRAMES - 1)
            norm_here = log_norm[clipped][:, :, None]
            dot_here = row_dots[clipped][:, :, None]
            prob = jnp.where(allowed(source, distance), jnp.exp(logits(queries, keys) - norm_here), 0.0)
            value_total = value_total + jnp.einsum("hij,ihc->jhc", to_half(prob), grads)
            grad_prob = jnp.einsum("ihc,jhc->hij", grads, split_heads(values))
            grad_score = to_half(prob * (grad_prob - dot_here))
            key_total = key_total + jnp.einsum("hij,ihc->jhc", grad_score, split_heads(queries))
        return ((scale * key_total).reshape(FRAME_TOK, D).astype(jnp.bfloat16),
                value_total.reshape(FRAME_TOK, D).astype(jnp.bfloat16))

    grad_query = lax.map(grad_queries, frames).reshape(TOKENS, D)
    key_part, value_part = lax.map(grad_keys, frames)
    return grad_query, key_part.reshape(TOKENS, D), value_part.reshape(TOKENS, D)
```

```python
import functools

import jax
import jax.numpy as jnp
from jax import lax
from jax.experimental import pallas as pl
from jax.experimental.pallas import tpu as pltpu
from jax.sharding import PartitionSpec as P

HEAD_DIM = 128


DISTANCES = (0, 1, 2, 4)
NEG_FILL = -1e30


def shifted(value, axis, by):
    peers = lax.axis_size(axis)
    pairs = [(i, i + by) for i in range(peers) if 0 <= i + by < peers]
    return lax.ppermute(value, axis, pairs)


def gathered_plan(
    grad_out, out_weight, row_owner, row_position, query_rows, key_rows, value_rows, band_widths
):
    frame_len = query_rows.shape[0]
    width = query_rows.shape[1]
    heads = width // HEAD_DIM
    scale = HEAD_DIM ** (-0.5)
    full_grad = lax.all_gather(grad_out, "head", axis=1, tiled=True)
    packed = jnp.einsum(
        "rc,hc->rh",
        full_grad,
        lax.all_gather(out_weight, "seq", axis=1, tiled=True),
        preferred_element_type=jnp.float32,
    ).astype(jnp.bfloat16)
    owners = lax.axis_size("seq")
    capacity = max(1, 3 * frame_len // (2 * owners))
    order_ids = jnp.arange(frame_len)
    same_owner = (row_owner[:, None] == row_owner[None, :]) & (
        order_ids[None, :] < order_ids[:, None]
    )
    earlier = jnp.sum(same_owner.astype(jnp.int32), axis=1)
    slot_ids = row_owner * capacity + earlier
    placing = jnp.arange(owners * capacity)[:, None] == slot_ids[None, :]
    outgoing = jnp.dot(placing.astype(jnp.bfloat16), packed, preferred_element_type=jnp.float32)
    outgoing = outgoing.astype(jnp.bfloat16).reshape(owners, capacity, width)
    slot_pos = (
        jnp.dot(
            placing.astype(jnp.float32),
            (row_position + 1).astype(jnp.float32),
            precision=lax.Precision.HIGHEST,
        )
        - 1.0
    )
    slot_pos = slot_pos.reshape(owners, capacity).astype(jnp.bfloat16)
    incoming, incoming_pos = (
        lax.all_to_all(outgoing, "seq", split_axis=0, concat_axis=0, tiled=True),
        lax.all_to_all(slot_pos, "seq", split_axis=0, concat_axis=0, tiled=True),
    )
    landing = (
        incoming_pos.reshape(-1).astype(jnp.float32)[None, :]
        == jnp.arange(frame_len, dtype=jnp.float32)[:, None]
    )
    grad_attn = jnp.dot(
        landing.astype(jnp.bfloat16),
        incoming.reshape(-1, width),
        preferred_element_type=jnp.float32,
    ).astype(jnp.bfloat16)
    frame = lax.axis_index("seq")
    remote = {}
    for distance in (1, 2, 4):
        remote[distance] = shifted((key_rows, value_rows), "seq", distance)
    remote[0] = (key_rows, value_rows)
    positions = jnp.arange(frame_len)
    spread = jnp.abs(positions[:, None] - positions[None, :])
    limits = {0: frame_len, 1: frame_len, 2: band_widths[0, 0], 4: band_widths[0, 1]}
    mask_list = [(frame - distance >= 0) & (spread < limits[distance]) for distance in DISTANCES]
    usable = jnp.concatenate(mask_list, axis=1)[None]
    key_all = jnp.concatenate([remote[distance][0] for distance in DISTANCES], axis=0)
    value_all = jnp.concatenate([remote[distance][1] for distance in DISTANCES], axis=0)
    key_heads = key_all.reshape(4 * frame_len, heads, HEAD_DIM)
    value_heads = value_all.reshape(4 * frame_len, heads, HEAD_DIM)
    query_heads = query_rows.reshape(frame_len, heads, HEAD_DIM)
    grad_heads = grad_attn.reshape(frame_len, heads, HEAD_DIM)
    scores = (
        jnp.einsum("ihc,jhc->hij", query_heads, key_heads, preferred_element_type=jnp.float32)
        * scale
    )
    row_max = jnp.max(jnp.where(usable, scores, NEG_FILL), axis=2, keepdims=True)
    weights = jnp.where(usable, jnp.exp(scores - row_max), 0.0)
    row_sum = jnp.sum(weights, axis=2, keepdims=True)
    attn_prob = weights / row_sum
    prob_half = attn_prob.astype(jnp.bfloat16)
    attn_out = jnp.einsum(
        "hij,jhc->ihc", prob_half, value_heads, preferred_element_type=jnp.float32
    )
    row_dot = jnp.sum(grad_heads.astype(jnp.float32) * attn_out, axis=2).T[:, :, None]
    grad_prob = jnp.einsum(
        "ihc,jhc->hij", grad_heads, value_heads, preferred_element_type=jnp.float32
    )
    grad_score = (attn_prob * (grad_prob - row_dot)).astype(jnp.bfloat16)
    grad_query = scale * jnp.einsum(
        "hij,jhc->ihc", grad_score, key_heads, preferred_element_type=jnp.float32
    )
    grad_query = grad_query.reshape(frame_len, width).astype(jnp.bfloat16)
    local_score = grad_score[:, :, :frame_len]
    local_half = prob_half[:, :, :frame_len]
    key_sum = scale * jnp.einsum(
        "hij,ihc->jhc", local_score, query_heads, preferred_element_type=jnp.float32
    )
    value_sum = jnp.einsum(
        "hij,ihc->jhc", local_half, grad_heads, preferred_element_type=jnp.float32
    )
    log_norm = (row_max + jnp.log(row_sum))[:, :, 0]
    stats_local = (log_norm, row_dot[:, :, 0], band_widths.astype(jnp.float32))
    own_keys = key_rows.reshape(frame_len, heads, HEAD_DIM)
    own_values = value_rows.reshape(frame_len, heads, HEAD_DIM)
    for distance in (1, 2, 4):
        query_recv, grad_recv = shifted((query_rows, grad_attn), "seq", -distance)
        norm_recv, dot_recv, band_recv = shifted(
            (stats_local[0], stats_local[1], stats_local[2]), "seq", -distance
        )
        if distance == 2:
            limit = band_recv[0, 0]
        elif distance == 4:
            limit = band_recv[0, 1]
        else:
            limit = jnp.float32(frame_len)
        valid = ((frame + distance < owners) & (spread.astype(jnp.float32) < limit))[None]
        query_far = query_recv.reshape(frame_len, heads, HEAD_DIM)
        grad_far = grad_recv.reshape(frame_len, heads, HEAD_DIM)
        far_scores = (
            jnp.einsum("ihc,jhc->hij", query_far, own_keys, preferred_element_type=jnp.float32)
            * scale
        )
        far_prob = jnp.where(valid, jnp.exp(far_scores - norm_recv[:, :, None]), 0.0)
        far_grad_prob = jnp.einsum(
            "ihc,jhc->hij", grad_far, own_values, preferred_element_type=jnp.float32
        )
        far_score = (far_prob * (far_grad_prob - dot_recv[:, :, None])).astype(jnp.bfloat16)
        key_sum = key_sum + scale * jnp.einsum(
            "hij,ihc->jhc", far_score, query_far, preferred_element_type=jnp.float32
        )
        value_sum = value_sum + jnp.einsum(
            "hij,ihc->jhc",
            far_prob.astype(jnp.bfloat16),
            grad_far,
            preferred_element_type=jnp.float32,
        )
    key_sum = key_sum.reshape(frame_len, width)
    value_sum = value_sum.reshape(frame_len, width)
    return (grad_query, key_sum.astype(jnp.bfloat16), value_sum.astype(jnp.bfloat16))


def dot(a, b, contract):
    return lax.dot_general(a, b, (contract, ((), ())), preferred_element_type=jnp.float32)


def fused_kernel(
    owners, groups,
    go, w, tgt, q, k, v, band,
    dq_out, dk_out, dv_out,
    grows, tall, xsend, xrecv, zsend, zrecv, own_part, kv, prob, half, attn, grad, score, part,
    back, total, send_sem, recv_sem,
):
    frame_len, width = q.shape
    depth = w.shape[1]
    heads = width // HEAD_DIM
    ratio = owners // groups
    shares = owners // groups
    pairs = owners // 2
    scale = HEAD_DIM ** (-0.5)
    s = lax.axis_index("seq")
    g = lax.axis_index("head")
    odd = lax.rem(s, 2)
    even = odd == 0
    peer = s + 1 - 2 * odd
    level = s // 2
    used = [0]
    pending = []

    def copy(src, dst, sem, ds, dg):
        used[0] += 1
        return pltpu.make_async_remote_copy(
            src_ref=src, dst_ref=dst, send_sem=send_sem.at[used[0] - 1], recv_sem=recv_sem.at[sem],
            device_id={"seq": ds, "head": dg}, device_id_type=pl.DeviceIdType.MESH,
        )

    def when(cond, action):
        if cond is None:
            action()
        else:
            pl.when(cond)(action)

    def send(cond, src, dst, sem, ds, dg):
        moving = copy(src, dst, sem, ds, dg)
        when(cond, lambda: moving.start())
        pending.append((cond, moving))

    def arrive(cond, dst, sem, ds, dg):
        moving = pltpu.make_async_remote_copy(
            src_ref=dst, dst_ref=dst, send_sem=send_sem.at[0], recv_sem=recv_sem.at[sem],
            device_id={"seq": ds, "head": dg}, device_id_type=pl.DeviceIdType.MESH,
        )
        when(cond, lambda: moving.wait_recv())

    sem_rows = 0
    sem_tgt = owners
    sem_x = 2 * owners
    sem_z = sem_x + pairs
    sem_kv = sem_z + pairs
    sem_back = sem_kv + 6

    relay = lax.rem(s, groups)
    source_group = s // ratio
    alone = (source_group == g) & (relay == g)

    barrier = pltpu.get_barrier_semaphore()

    def greet(ds, dg):
        pl.semaphore_signal(
            barrier, inc=1, device_id={"seq": ds, "head": dg}, device_id_type=pl.DeviceIdType.MESH
        )

    for i in range(1, owners):
        greet(lax.rem(s + i, owners), g)
    for i in range(1, groups):
        greet(s, lax.rem(g + i, groups))
    for i in range(ratio):
        ds = ratio * g + i
        pl.when((ds != s) | (relay != g))(functools.partial(greet, ds, relay))
    for i in range(shares):
        origin = g + i * groups
        pl.when((origin != s) | (source_group != g))(functools.partial(greet, origin, source_group))
    greetings = owners - 1 + groups - 1 + ratio + shares
    pl.semaphore_wait(barrier, jnp.where(alone, greetings - 2, greetings))

    for i in range(ratio):
        ds = ratio * g + i
        own = (ds == s) & (relay == g)
        block = go.at[:, pl.ds(i * depth, depth)]

        def keep(block=block):
            grows[s] = block[...]

        pl.when(own)(keep)
        send(jnp.logical_not(own), block, grows.at[s], sem_rows + s, ds, relay)
    tall[s] = tgt[...]
    for i in range(1, owners):
        send(None, tgt, tall.at[s], sem_tgt + s, lax.rem(s + i, owners), g)

    has_two = s + 2 < owners
    for j, ref in enumerate((k, v)):
        send(has_two, ref, kv.at[1, j], sem_kv + 2 + j, jnp.minimum(s + 2, owners - 1), g)
    for j, ref in enumerate((k, v)):
        send(even, ref, kv.at[0, j], sem_kv + j, peer, g)

    def clear(slot):
        kv[slot] = jnp.zeros((2, frame_len, width), jnp.bfloat16)

    pl.when(s < 1)(lambda: clear(0))
    pl.when(s < 2)(lambda: clear(1))
    pl.when(s < 4)(lambda: clear(2))

    for i in range(shares):
        origin = g + i * groups
        own = (origin == s) & (source_group == g)
        arrive(jnp.logical_not(own), grows.at[origin], sem_rows + origin, origin, source_group)
        for j in range(1, groups):
            send(None, grows.at[origin], grows.at[origin], sem_rows + origin, s, lax.rem(g + j, groups))
    for j in range(1, groups):
        via = lax.rem(g + j, groups)
        for i in range(shares):
            origin = via + i * groups
            arrive(None, grows.at[origin], sem_rows + origin, s, via)
    for i in range(1, owners):
        origin = lax.rem(s + i, owners)
        arrive(None, tall.at[origin], sem_tgt + origin, origin, g)

    has_back = s >= 2
    behind = jnp.maximum(s - 2, 0)
    ahead = jnp.minimum(s + 2, owners - 1)
    for j in range(2):
        arrive(has_back, kv.at[1, j], sem_kv + 2 + j, behind, g)
    for j in range(2):
        send(has_back & has_two, kv.at[1, j], kv.at[2, j], sem_kv + 4 + j, ahead, g)
    for j in range(2):
        send(has_back & (odd == 1), kv.at[1, j], kv.at[0, j], sem_kv + j, peer, g)

    row_ids = lax.broadcasted_iota(jnp.int32, (frame_len, frame_len), 0)

    def partials(parity):
        picks = []
        for z in range(pairs):
            frame = 2 * z + parity
            picks.append(
                jnp.concatenate(
                    [
                        jnp.where(tall[o, 0:1, :] == row_ids + frame * frame_len, 1.0, 0.0).astype(jnp.bfloat16)
                        for o in range(owners)
                    ],
                    axis=1,
                )
            )
        pick = jnp.concatenate(picks, axis=0)
        rows = dot(pick, grows[...].reshape(owners * frame_len, depth), ((1,), (0,)))
        return dot(rows.astype(jnp.bfloat16), w[...], ((1,), (1,)))

    far = partials(1 - odd)
    for z in range(pairs):
        xsend[z] = far[z * frame_len:(z + 1) * frame_len].astype(jnp.bfloat16)
    for i in range(pairs):
        z = lax.rem(level + 1 + i, pairs)
        send(None, xsend.at[z], xrecv.at[z], sem_x + z, peer, g)
    own_part[...] = partials(odd).reshape(pairs, frame_len, width)
    for i in range(pairs):
        z = lax.rem(level + 1 + i, pairs)
        arrive(None, xrecv.at[z], sem_x + z, peer, g)
        summed = (own_part[z] + xrecv[z].astype(jnp.float32)).astype(jnp.bfloat16)
        if i < pairs - 1:
            zsend[z] = summed
            send(None, zsend.at[z], zrecv.at[level], sem_z + level, 2 * z + odd, g)
        else:
            zrecv[z] = summed

    has_one = s >= 1
    has_four = s >= 4
    for j in range(2):
        arrive(has_one, kv.at[0, j], sem_kv + j, peer, g)
    for j in range(2):
        arrive(has_four, kv.at[2, j], sem_kv + 4 + j, behind, g)
    spread = jnp.abs(row_ids - lax.broadcasted_iota(jnp.int32, (frame_len, frame_len), 1))
    limits = (
        frame_len,
        jnp.where(s >= 1, frame_len, 0),
        jnp.where(s >= 2, band[0, 0], 0),
        jnp.where(s >= 4, band[0, 1], 0),
    )
    masks = [spread < limit for limit in limits]

    def lanes(h):
        return slice(h * HEAD_DIM, (h + 1) * HEAD_DIM)

    def tokens(d):
        return slice(d * frame_len, (d + 1) * frame_len)

    def far_heads(j, ref, h):
        return [ref[:, lanes(h)]] + [kv[d, j, :, lanes(h)] for d in range(3)]

    for h in range(heads):
        qh = q[:, lanes(h)]
        keys = jnp.concatenate(far_heads(0, k, h), axis=0)
        values = jnp.concatenate(far_heads(1, v, h), axis=0)
        usable = jnp.concatenate([jnp.where(m, 1.0, 0.0) for m in masks], axis=1) > 0.5
        scores = dot(qh, keys, ((1,), (1,))) * scale
        row_max = jnp.max(jnp.where(usable, scores, NEG_FILL), axis=1, keepdims=True)
        weights = jnp.where(usable, jnp.exp(scores - row_max), 0.0)
        probs = weights / jnp.sum(weights, axis=1, keepdims=True)
        prob[h] = probs
        half[h] = probs.astype(jnp.bfloat16)
        attn[h] = dot(probs.astype(jnp.bfloat16), values, ((1,), (0,)))

    for i in range(1, pairs):
        z = lax.rem(level + i, pairs)
        arrive(None, zrecv.at[z], sem_z + z, 2 * z + odd, g)
    grad[...] = sum(zrecv[z].astype(jnp.float32) for z in range(pairs)).astype(jnp.bfloat16)

    for h in range(heads):
        gh = grad[:, lanes(h)]
        values = jnp.concatenate(far_heads(1, v, h), axis=0)
        row_dot = jnp.sum(gh.astype(jnp.float32) * attn[h], axis=1, keepdims=True)
        grad_prob = dot(gh, values, ((1,), (1,)))
        score[h] = (prob[h] * (grad_prob - row_dot)).astype(jnp.bfloat16)

    def key_part(h, d):
        return dot(score[h, :, tokens(d)], q[:, lanes(h)], ((0,), (0,)))

    def value_part(h, d):
        return dot(half[h, :, tokens(d)], grad[:, lanes(h)], ((0,), (0,)))

    for h in range(heads):
        part[0, 0, :, lanes(h)] = key_part(h, 3).astype(jnp.bfloat16)
        part[0, 1, :, lanes(h)] = value_part(h, 3).astype(jnp.bfloat16)
    for j in range(2):
        send(has_four, part.at[0, j], back.at[0, j], sem_back + j, behind, g)
    for h in range(heads):
        part[1, 0, :, lanes(h)] = key_part(h, 1).astype(jnp.bfloat16)
        part[1, 1, :, lanes(h)] = value_part(h, 1).astype(jnp.bfloat16)
    for j in range(2):
        send(has_one, part.at[1, j], back.at[1, j], sem_back + 2 + j, peer, g)
    for h in range(heads):
        total[0, :, lanes(h)] = key_part(h, 2)
        total[1, :, lanes(h)] = value_part(h, 2)

    def add(slot):
        for j in range(2):
            total[j] += back[slot, j].astype(jnp.float32)

    passed = has_back & has_two
    for j in range(2):
        arrive(passed, back.at[0, j], sem_back + j, ahead, g)
    pl.when(passed)(lambda: add(0))
    for j in range(2):
        arrive((odd == 0) | (s >= 3), back.at[1, j], sem_back + 2 + j, peer, g)
    pl.when((odd == 1) & (s >= 3))(lambda: add(1))
    for j in range(2):
        part[2, j] = total[j].astype(jnp.bfloat16)
    for j in range(2):
        send(has_back, part.at[2, j], back.at[2, j], sem_back + 4 + j, behind, g)

    for h in range(heads):
        total[0, :, lanes(h)] = key_part(h, 0)
        total[1, :, lanes(h)] = value_part(h, 0)
        keys = jnp.concatenate(far_heads(0, k, h), axis=0)
        dq_out[:, lanes(h)] = (scale * dot(score[h], keys, ((1,), (0,)))).astype(jnp.bfloat16)
    pl.when(even)(lambda: add(1))
    for j in range(2):
        arrive(has_two, back.at[2, j], sem_back + 4 + j, ahead, g)
    pl.when(has_two)(lambda: add(2))
    dk_out[...] = (scale * total[0]).astype(jnp.bfloat16)
    dv_out[...] = total[1].astype(jnp.bfloat16)
    for cond, moving in pending:
        when(cond, lambda moving=moving: moving.wait_send())


def fused_plan(
    grad_out, out_weight, row_owner, row_position, query_rows, key_rows, value_rows, band_widths
):
    owners = lax.axis_size("seq")
    groups = lax.axis_size("head")
    frame_len, width = query_rows.shape
    depth = out_weight.shape[1]
    heads = width // HEAD_DIM
    pairs = owners // 2
    target = jnp.broadcast_to((row_owner * frame_len + row_position)[None, :], (8, frame_len))
    half = jnp.bfloat16
    vmem = pl.BlockSpec(memory_space=pltpu.VMEM)
    out = jax.ShapeDtypeStruct((frame_len, width), half)
    return pl.pallas_call(
        functools.partial(fused_kernel, owners, groups),
        out_shape=(out, out, out),
        in_specs=[vmem] * 6 + [pl.BlockSpec(memory_space=pltpu.SMEM)],
        out_specs=(vmem, vmem, vmem),
        scratch_shapes=[
            pltpu.VMEM((owners, frame_len, depth), half),
            pltpu.VMEM((owners, 8, frame_len), jnp.int32),
            pltpu.VMEM((pairs, frame_len, width), half),
            pltpu.VMEM((pairs, frame_len, width), half),
            pltpu.VMEM((pairs, frame_len, width), half),
            pltpu.VMEM((pairs, frame_len, width), half),
            pltpu.VMEM((pairs, frame_len, width), jnp.float32),
            pltpu.VMEM((3, 2, frame_len, width), half),
            pltpu.VMEM((heads, frame_len, 4 * frame_len), jnp.float32),
            pltpu.VMEM((heads, frame_len, 4 * frame_len), half),
            pltpu.VMEM((heads, frame_len, HEAD_DIM), jnp.float32),
            pltpu.VMEM((frame_len, width), half),
            pltpu.VMEM((heads, frame_len, 4 * frame_len), half),
            pltpu.VMEM((3, 2, frame_len, width), half),
            pltpu.VMEM((3, 2, frame_len, width), half),
            pltpu.VMEM((2, frame_len, width), jnp.float32),
            pltpu.SemaphoreType.DMA((96,)),
            pltpu.SemaphoreType.DMA((3 * owners + 12,)),
        ],
        compiler_params=pltpu.CompilerParams(
            collective_id=0, has_side_effects=True, vmem_limit_bytes=40 * 1024 * 1024
        ),
    )(grad_out, out_weight, target, query_rows, key_rows, value_rows, band_widths)


def per_device(
    grad_out, out_weight, row_owner, row_position, query_rows, key_rows, value_rows, band_widths
):
    owners = lax.axis_size("seq")
    groups = lax.axis_size("head")
    rows, width = query_rows.shape
    depth = out_weight.shape[1]
    model = owners * depth
    by_partials = owners * rows * (width + depth)
    by_weights = model * (width + rows)
    fits = owners % 2 == 0 and owners >= 4 and owners % groups == 0 and depth % 128 == 0
    plan = fused_plan if fits and rows % 128 == 0 and by_partials < by_weights else gathered_plan
    return plan(
        grad_out, out_weight, row_owner, row_position, query_rows, key_rows, value_rows, band_widths
    )


def solution(mesh):
    return jax.shard_map(
        per_device,
        mesh=mesh,
        in_specs=(
            P("seq", "head"),
            P("head", "seq"),
            P("seq"),
            P("seq"),
            P("seq", "head"),
            P("seq", "head"),
            P("seq", "head"),
            P("seq", None),
        ),
        out_specs=(P("seq", "head"), P("seq", "head"), P("seq", "head")),
        check_vma=False,
    )
```

```python
import functools

import jax
import jax.numpy as jnp
from jax import lax
from jax.experimental import pallas as pl
from jax.experimental.pallas import tpu as pltpu
from jax.sharding import PartitionSpec as P

HEAD_DIM = 128


DISTANCES = (0, 1, 2, 4)
NEG_FILL = -1e30


def shifted(value, axis, by):
    peers = lax.axis_size(axis)
    pairs = [(i, i + by) for i in range(peers) if 0 <= i + by < peers]
    return lax.ppermute(value, axis, pairs)


def gathered_plan(
    grad_out, out_weight, row_owner, row_position, query_rows, key_rows, value_rows, band_widths
):
    frame_len = query_rows.shape[0]
    width = query_rows.shape[1]
    heads = width // HEAD_DIM
    scale = HEAD_DIM ** (-0.5)
    full_grad = lax.all_gather(grad_out, "head", axis=1, tiled=True)
    packed = jnp.einsum(
        "rc,hc->rh",
        full_grad,
        lax.all_gather(out_weight, "seq", axis=1, tiled=True),
        preferred_element_type=jnp.float32,
    ).astype(jnp.bfloat16)
    owners = lax.axis_size("seq")
    capacity = max(1, 3 * frame_len // (2 * owners))
    order_ids = jnp.arange(frame_len)
    same_owner = (row_owner[:, None] == row_owner[None, :]) & (
        order_ids[None, :] < order_ids[:, None]
    )
    earlier = jnp.sum(same_owner.astype(jnp.int32), axis=1)
    slot_ids = row_owner * capacity + earlier
    placing = jnp.arange(owners * capacity)[:, None] == slot_ids[None, :]
    outgoing = jnp.dot(placing.astype(jnp.bfloat16), packed, preferred_element_type=jnp.float32)
    outgoing = outgoing.astype(jnp.bfloat16).reshape(owners, capacity, width)
    slot_pos = (
        jnp.dot(
            placing.astype(jnp.float32),
            (row_position + 1).astype(jnp.float32),
            precision=lax.Precision.HIGHEST,
        )
        - 1.0
    )
    slot_pos = slot_pos.reshape(owners, capacity).astype(jnp.bfloat16)
    incoming, incoming_pos = (
        lax.all_to_all(outgoing, "seq", split_axis=0, concat_axis=0, tiled=True),
        lax.all_to_all(slot_pos, "seq", split_axis=0, concat_axis=0, tiled=True),
    )
    landing = (
        incoming_pos.reshape(-1).astype(jnp.float32)[None, :]
        == jnp.arange(frame_len, dtype=jnp.float32)[:, None]
    )
    grad_attn = jnp.dot(
        landing.astype(jnp.bfloat16),
        incoming.reshape(-1, width),
        preferred_element_type=jnp.float32,
    ).astype(jnp.bfloat16)
    frame = lax.axis_index("seq")
    remote = {}
    for distance in (1, 2, 4):
        remote[distance] = shifted((key_rows, value_rows), "seq", distance)
    remote[0] = (key_rows, value_rows)
    positions = jnp.arange(frame_len)
    spread = jnp.abs(positions[:, None] - positions[None, :])
    limits = {0: frame_len, 1: frame_len, 2: band_widths[0, 0], 4: band_widths[0, 1]}
    mask_list = [(frame - distance >= 0) & (spread < limits[distance]) for distance in DISTANCES]
    usable = jnp.concatenate(mask_list, axis=1)[None]
    key_all = jnp.concatenate([remote[distance][0] for distance in DISTANCES], axis=0)
    value_all = jnp.concatenate([remote[distance][1] for distance in DISTANCES], axis=0)
    key_heads = key_all.reshape(4 * frame_len, heads, HEAD_DIM)
    value_heads = value_all.reshape(4 * frame_len, heads, HEAD_DIM)
    query_heads = query_rows.reshape(frame_len, heads, HEAD_DIM)
    grad_heads = grad_attn.reshape(frame_len, heads, HEAD_DIM)
    scores = (
        jnp.einsum("ihc,jhc->hij", query_heads, key_heads, preferred_element_type=jnp.float32)
        * scale
    )
    row_max = jnp.max(jnp.where(usable, scores, NEG_FILL), axis=2, keepdims=True)
    weights = jnp.where(usable, jnp.exp(scores - row_max), 0.0)
    row_sum = jnp.sum(weights, axis=2, keepdims=True)
    attn_prob = weights / row_sum
    prob_half = attn_prob.astype(jnp.bfloat16)
    attn_out = jnp.einsum(
        "hij,jhc->ihc", prob_half, value_heads, preferred_element_type=jnp.float32
    )
    row_dot = jnp.sum(grad_heads.astype(jnp.float32) * attn_out, axis=2).T[:, :, None]
    grad_prob = jnp.einsum(
        "ihc,jhc->hij", grad_heads, value_heads, preferred_element_type=jnp.float32
    )
    grad_score = (attn_prob * (grad_prob - row_dot)).astype(jnp.bfloat16)
    grad_query = scale * jnp.einsum(
        "hij,jhc->ihc", grad_score, key_heads, preferred_element_type=jnp.float32
    )
    grad_query = grad_query.reshape(frame_len, width).astype(jnp.bfloat16)
    local_score = grad_score[:, :, :frame_len]
    local_half = prob_half[:, :, :frame_len]
    key_sum = scale * jnp.einsum(
        "hij,ihc->jhc", local_score, query_heads, preferred_element_type=jnp.float32
    )
    value_sum = jnp.einsum(
        "hij,ihc->jhc", local_half, grad_heads, preferred_element_type=jnp.float32
    )
    log_norm = (row_max + jnp.log(row_sum))[:, :, 0]
    stats_local = (log_norm, row_dot[:, :, 0], band_widths.astype(jnp.float32))
    own_keys = key_rows.reshape(frame_len, heads, HEAD_DIM)
    own_values = value_rows.reshape(frame_len, heads, HEAD_DIM)
    for distance in (1, 2, 4):
        query_recv, grad_recv = shifted((query_rows, grad_attn), "seq", -distance)
        norm_recv, dot_recv, band_recv = shifted(
            (stats_local[0], stats_local[1], stats_local[2]), "seq", -distance
        )
        if distance == 2:
            limit = band_recv[0, 0]
        elif distance == 4:
            limit = band_recv[0, 1]
        else:
            limit = jnp.float32(frame_len)
        valid = ((frame + distance < owners) & (spread.astype(jnp.float32) < limit))[None]
        query_far = query_recv.reshape(frame_len, heads, HEAD_DIM)
        grad_far = grad_recv.reshape(frame_len, heads, HEAD_DIM)
        far_scores = (
            jnp.einsum("ihc,jhc->hij", query_far, own_keys, preferred_element_type=jnp.float32)
            * scale
        )
        far_prob = jnp.where(valid, jnp.exp(far_scores - norm_recv[:, :, None]), 0.0)
        far_grad_prob = jnp.einsum(
            "ihc,jhc->hij", grad_far, own_values, preferred_element_type=jnp.float32
        )
        far_score = (far_prob * (far_grad_prob - dot_recv[:, :, None])).astype(jnp.bfloat16)
        key_sum = key_sum + scale * jnp.einsum(
            "hij,ihc->jhc", far_score, query_far, preferred_element_type=jnp.float32
        )
        value_sum = value_sum + jnp.einsum(
            "hij,ihc->jhc",
            far_prob.astype(jnp.bfloat16),
            grad_far,
            preferred_element_type=jnp.float32,
        )
    key_sum = key_sum.reshape(frame_len, width)
    value_sum = value_sum.reshape(frame_len, width)
    return (grad_query, key_sum.astype(jnp.bfloat16), value_sum.astype(jnp.bfloat16))


def dot(a, b, contract):
    return lax.dot_general(a, b, (contract, ((), ())), preferred_element_type=jnp.float32)


def fused_kernel(
    owners, groups,
    go_in, w_in, info, q_in, k_in, v_in, band,
    dq_out, dk_out, dv_out,
    go, wpair, q, k, v, rsend, grows, codes, tall, zsend, zrecv, kv, prob, half, attn, grad, score,
    part, back, total, send_sem, recv_sem, load_sem,
):
    frame_len, width = q.shape
    depth = w_in.shape[1]
    cap = rsend.shape[1]
    heads = width // HEAD_DIM
    ratio = owners // groups
    shares = owners // groups
    pairs = owners // 2
    scale = HEAD_DIM ** (-0.5)
    s = lax.axis_index("seq")
    g = lax.axis_index("head")
    odd = lax.rem(s, 2)
    even = odd == 0
    peer = s + 1 - 2 * odd
    level = s // 2
    used = [0]
    pending = []

    def copy(src, dst, sem, ds, dg):
        used[0] += 1
        return pltpu.make_async_remote_copy(
            src_ref=src, dst_ref=dst, send_sem=send_sem.at[used[0] - 1], recv_sem=recv_sem.at[sem],
            device_id={"seq": ds, "head": dg}, device_id_type=pl.DeviceIdType.MESH,
        )

    def when(cond, action):
        if cond is None:
            action()
        else:
            pl.when(cond)(action)

    def send(cond, src, dst, sem, ds, dg):
        moving = copy(src, dst, sem, ds, dg)
        when(cond, lambda: moving.start())
        pending.append((cond, moving))

    def arrive(cond, dst, sem, ds, dg):
        moving = pltpu.make_async_remote_copy(
            src_ref=dst, dst_ref=dst, send_sem=send_sem.at[0], recv_sem=recv_sem.at[sem],
            device_id={"seq": ds, "head": dg}, device_id_type=pl.DeviceIdType.MESH,
        )
        when(cond, lambda: moving.wait_recv())

    sem_rows = 0
    sem_tgt = owners
    sem_w = 2 * owners
    sem_z = sem_w + 1
    sem_kv = sem_z + pairs
    sem_back = sem_kv + 6

    relay = lax.rem(s, groups)
    source_group = s // ratio
    alone = (source_group == g) & (relay == g)

    barrier = pltpu.get_barrier_semaphore()

    def greet(ds, dg):
        pl.semaphore_signal(
            barrier, inc=1, device_id={"seq": ds, "head": dg}, device_id_type=pl.DeviceIdType.MESH
        )

    for i in range(1, owners):
        greet(lax.rem(s + i, owners), g)
    for i in range(1, groups):
        greet(s, lax.rem(g + i, groups))
    for i in range(ratio):
        ds = ratio * g + i
        pl.when((ds != s) | (relay != g))(functools.partial(greet, ds, relay))
    for i in range(shares):
        origin = g + i * groups
        pl.when((origin != s) | (source_group != g))(functools.partial(greet, origin, source_group))
    loads = [
        pltpu.make_async_copy(src, dst, load_sem.at[i])
        for i, (src, dst) in enumerate(
            ((go_in, go), (k_in, k), (v_in, v), (q_in, q), (w_in, wpair.at[odd]))
        )
    ]
    for moving in loads:
        moving.start()

    row_ids = lax.broadcasted_iota(jnp.int32, (frame_len, frame_len), 0)
    col_ids = lax.broadcasted_iota(jnp.int32, (frame_len, frame_len), 1)
    earlier = jnp.where(row_ids < col_ids, 1.0, 0.0).astype(jnp.bfloat16)
    chosen = []
    for parity in range(2):
        member = jnp.where(info[2] == parity, 1.0, 0.0)
        rank = dot(member.astype(jnp.bfloat16), earlier, ((1,), (0,)))
        slot = jnp.where(member > 0.5, rank, -1.0)[0:1]
        choose = jnp.where(row_ids.astype(jnp.float32) == slot, 1.0, 0.0).astype(jnp.bfloat16)
        owner = dot(info[0].astype(jnp.bfloat16), choose, ((1,), (1,)))
        place = dot(info[1].astype(jnp.bfloat16), choose, ((1,), (1,)))
        codes[parity] = (owner - 1.0) * frame_len + place
        chosen.append(choose[:cap])
    loads[0].wait()
    for parity in range(2):
        rsend[parity] = dot(chosen[parity], go[...], ((1,), (0,))).astype(jnp.bfloat16)

    greetings = owners - 1 + groups - 1 + ratio + shares
    pl.semaphore_wait(barrier, jnp.where(alone, greetings - 2, greetings))

    for i in range(ratio):
        ds = ratio * g + i
        own = (ds == s) & (relay == g)

        def keep(i=i):
            grows[s] = rsend[i]

        pl.when(own)(keep)
        send(jnp.logical_not(own), rsend.at[i], grows.at[s], sem_rows + s, ds, relay)
    tall[s] = codes[odd]
    for i in range(1, owners):
        ds = lax.rem(s + i, owners)
        send(None, codes.at[lax.rem(ds, 2)], tall.at[s], sem_tgt + s, ds, g)
    send(None, w_in, wpair.at[odd], sem_w, peer, g)

    has_two = s + 2 < owners
    for j, ref in enumerate((k_in, v_in)):
        send(has_two, ref, kv.at[1, j], sem_kv + 2 + j, jnp.minimum(s + 2, owners - 1), g)
    for j, ref in enumerate((k_in, v_in)):
        send(even, ref, kv.at[0, j], sem_kv + j, peer, g)

    def clear(slot):
        kv[slot] = jnp.zeros((2, frame_len, width), jnp.bfloat16)

    pl.when(s < 1)(lambda: clear(0))
    pl.when(s < 2)(lambda: clear(1))
    pl.when(s < 4)(lambda: clear(2))

    for i in range(shares):
        origin = g + i * groups
        own = (origin == s) & (source_group == g)
        arrive(jnp.logical_not(own), grows.at[origin], sem_rows + origin, origin, source_group)
        for j in range(1, groups):
            send(None, grows.at[origin], grows.at[origin], sem_rows + origin, s, lax.rem(g + j, groups))
    for j in range(1, groups):
        via = lax.rem(g + j, groups)
        for i in range(shares):
            origin = via + i * groups
            arrive(None, grows.at[origin], sem_rows + origin, s, via)
    for i in range(1, owners):
        origin = lax.rem(s + i, owners)
        arrive(None, tall.at[origin], sem_tgt + origin, origin, g)

    has_back = s >= 2
    behind = jnp.maximum(s - 2, 0)
    ahead = jnp.minimum(s + 2, owners - 1)
    for j in range(2):
        arrive(has_back, kv.at[1, j], sem_kv + 2 + j, behind, g)
    for j in range(2):
        send(has_back & has_two, kv.at[1, j], kv.at[2, j], sem_kv + 4 + j, ahead, g)
    for j in range(2):
        send(has_back & (odd == 1), kv.at[1, j], kv.at[0, j], sem_kv + j, peer, g)

    for moving in loads[1:]:
        moving.wait()
    arrive(None, wpair.at[1 - odd], sem_w, peer, g)
    code = jnp.concatenate([tall[o][:, :cap] for o in range(owners)], axis=1)[0:1]
    lane_rows = lax.broadcasted_iota(jnp.int32, (frame_len, owners * cap), 0)
    pick = jnp.concatenate(
        [
            jnp.where(
                code == (lane_rows + (2 * z + odd) * frame_len).astype(jnp.float32), 1.0, 0.0
            ).astype(jnp.bfloat16)
            for z in range(pairs)
        ],
        axis=0,
    )
    rows = dot(pick, grows[...].reshape(owners * cap, width), ((1,), (0,))).astype(jnp.bfloat16)
    sums = dot(rows[:, :depth], wpair[0], ((1,), (1,))) + dot(rows[:, depth:], wpair[1], ((1,), (1,)))
    zsend[...] = sums.astype(jnp.bfloat16).reshape(pairs, frame_len, width)
    for i in range(1, pairs):
        z = lax.rem(level + i, pairs)
        send(None, zsend.at[z], zrecv.at[level], sem_z + level, 2 * z + odd, g)
    zrecv[level] = zsend[level]

    has_one = s >= 1
    has_four = s >= 4
    for j in range(2):
        arrive(has_one, kv.at[0, j], sem_kv + j, peer, g)
    for j in range(2):
        arrive(has_four, kv.at[2, j], sem_kv + 4 + j, behind, g)
    spread = jnp.abs(row_ids - col_ids)
    limits = (
        frame_len,
        jnp.where(s >= 1, frame_len, 0),
        jnp.where(s >= 2, band[0, 0], 0),
        jnp.where(s >= 4, band[0, 1], 0),
    )
    masks = [spread < limit for limit in limits]

    def lanes(h):
        return slice(h * HEAD_DIM, (h + 1) * HEAD_DIM)

    def tokens(d):
        return slice(d * frame_len, (d + 1) * frame_len)

    def far_heads(j, ref, h):
        return [ref[:, lanes(h)]] + [kv[d, j, :, lanes(h)] for d in range(3)]

    for h in range(heads):
        qh = q[:, lanes(h)]
        keys = jnp.concatenate(far_heads(0, k, h), axis=0)
        values = jnp.concatenate(far_heads(1, v, h), axis=0)
        usable = jnp.concatenate([jnp.where(m, 1.0, 0.0) for m in masks], axis=1) > 0.5
        scores = dot(qh, keys, ((1,), (1,))) * scale
        row_max = jnp.max(jnp.where(usable, scores, NEG_FILL), axis=1, keepdims=True)
        weights = jnp.where(usable, jnp.exp(scores - row_max), 0.0)
        probs = weights / jnp.sum(weights, axis=1, keepdims=True)
        prob[h] = probs
        half[h] = probs.astype(jnp.bfloat16)
        attn[h] = dot(probs.astype(jnp.bfloat16), values, ((1,), (0,)))

    for i in range(1, pairs):
        z = lax.rem(level + i, pairs)
        arrive(None, zrecv.at[z], sem_z + z, 2 * z + odd, g)
    grad[...] = sum(zrecv[z].astype(jnp.float32) for z in range(pairs)).astype(jnp.bfloat16)

    for h in range(heads):
        gh = grad[:, lanes(h)]
        values = jnp.concatenate(far_heads(1, v, h), axis=0)
        row_dot = jnp.sum(gh.astype(jnp.float32) * attn[h], axis=1, keepdims=True)
        grad_prob = dot(gh, values, ((1,), (1,)))
        score[h] = (prob[h] * (grad_prob - row_dot)).astype(jnp.bfloat16)

    def key_part(h, d):
        return dot(score[h, :, tokens(d)], q[:, lanes(h)], ((0,), (0,)))

    def value_part(h, d):
        return dot(half[h, :, tokens(d)], grad[:, lanes(h)], ((0,), (0,)))

    for h in range(heads):
        part[0, 0, :, lanes(h)] = key_part(h, 3).astype(jnp.bfloat16)
        part[0, 1, :, lanes(h)] = value_part(h, 3).astype(jnp.bfloat16)
    for j in range(2):
        send(has_four, part.at[0, j], back.at[0, j], sem_back + j, behind, g)
    for h in range(heads):
        part[1, 0, :, lanes(h)] = key_part(h, 1).astype(jnp.bfloat16)
        part[1, 1, :, lanes(h)] = value_part(h, 1).astype(jnp.bfloat16)
    for j in range(2):
        send(has_one, part.at[1, j], back.at[1, j], sem_back + 2 + j, peer, g)
    for h in range(heads):
        total[0, :, lanes(h)] = key_part(h, 2)
        total[1, :, lanes(h)] = value_part(h, 2)

    def add(slot):
        for j in range(2):
            total[j] += back[slot, j].astype(jnp.float32)

    passed = has_back & has_two
    for j in range(2):
        arrive(passed, back.at[0, j], sem_back + j, ahead, g)
    pl.when(passed)(lambda: add(0))
    for j in range(2):
        arrive((odd == 0) | (s >= 3), back.at[1, j], sem_back + 2 + j, peer, g)
    pl.when((odd == 1) & (s >= 3))(lambda: add(1))
    for j in range(2):
        part[2, j] = total[j].astype(jnp.bfloat16)
    for j in range(2):
        send(has_back, part.at[2, j], back.at[2, j], sem_back + 4 + j, behind, g)

    for h in range(heads):
        total[0, :, lanes(h)] = key_part(h, 0)
        total[1, :, lanes(h)] = value_part(h, 0)
        keys = jnp.concatenate(far_heads(0, k, h), axis=0)
        dq_out[:, lanes(h)] = (scale * dot(score[h], keys, ((1,), (0,)))).astype(jnp.bfloat16)
    pl.when(even)(lambda: add(1))
    for j in range(2):
        arrive(has_two, back.at[2, j], sem_back + 4 + j, ahead, g)
    pl.when(has_two)(lambda: add(2))
    dk_out[...] = (scale * total[0]).astype(jnp.bfloat16)
    dv_out[...] = total[1].astype(jnp.bfloat16)
    for cond, moving in pending:
        when(cond, lambda moving=moving: moving.wait_send())


def fused_plan(
    grad_out, out_weight, row_owner, row_position, query_rows, key_rows, value_rows, band_widths
):
    owners = lax.axis_size("seq")
    groups = lax.axis_size("head")
    frame_len, width = query_rows.shape
    depth = out_weight.shape[1]
    heads = width // HEAD_DIM
    pairs = owners // 2
    cap = pairs * max(1, 3 * frame_len // (2 * owners))
    cap = min(frame_len, -(-cap // 16) * 16)
    info = jnp.stack([row_owner + 1, row_position, row_owner % 2]).astype(jnp.float32)
    info = jnp.broadcast_to(info[:, None, :], (3, 8, frame_len))
    half = jnp.bfloat16
    vmem = pl.BlockSpec(memory_space=pltpu.VMEM)
    hbm = pl.BlockSpec(memory_space=pltpu.HBM)
    out = jax.ShapeDtypeStruct((frame_len, width), half)
    return pl.pallas_call(
        functools.partial(fused_kernel, owners, groups),
        out_shape=(out, out, out),
        in_specs=[hbm, hbm, vmem, hbm, hbm, hbm, pl.BlockSpec(memory_space=pltpu.SMEM)],
        out_specs=(vmem, vmem, vmem),
        scratch_shapes=[
            pltpu.VMEM((frame_len, width), half),
            pltpu.VMEM((2, width, depth), half),
            pltpu.VMEM((frame_len, width), half),
            pltpu.VMEM((frame_len, width), half),
            pltpu.VMEM((frame_len, width), half),
            pltpu.VMEM((2, cap, width), half),
            pltpu.VMEM((owners, cap, width), half),
            pltpu.VMEM((2, 8, frame_len), jnp.float32),
            pltpu.VMEM((owners, 8, frame_len), jnp.float32),
            pltpu.VMEM((pairs, frame_len, width), half),
            pltpu.VMEM((pairs, frame_len, width), half),
            pltpu.VMEM((3, 2, frame_len, width), half),
            pltpu.VMEM((heads, frame_len, 4 * frame_len), jnp.float32),
            pltpu.VMEM((heads, frame_len, 4 * frame_len), half),
            pltpu.VMEM((heads, frame_len, HEAD_DIM), jnp.float32),
            pltpu.VMEM((frame_len, width), half),
            pltpu.VMEM((heads, frame_len, 4 * frame_len), half),
            pltpu.VMEM((3, 2, frame_len, width), half),
            pltpu.VMEM((3, 2, frame_len, width), half),
            pltpu.VMEM((2, frame_len, width), jnp.float32),
            pltpu.SemaphoreType.DMA((96,)),
            pltpu.SemaphoreType.DMA((3 * owners + 13,)),
            pltpu.SemaphoreType.DMA((5,)),
        ],
        compiler_params=pltpu.CompilerParams(
            collective_id=0, has_side_effects=True, vmem_limit_bytes=40 * 1024 * 1024
        ),
    )(grad_out, out_weight, info, query_rows, key_rows, value_rows, band_widths)


def per_device(
    grad_out, out_weight, row_owner, row_position, query_rows, key_rows, value_rows, band_widths
):
    owners = lax.axis_size("seq")
    groups = lax.axis_size("head")
    rows, width = query_rows.shape
    depth = out_weight.shape[1]
    model = owners * depth
    by_partials = owners * rows * width
    by_weights = model * (width + rows)
    fits = owners == 2 * groups and owners >= 4 and depth % 128 == 0
    plan = fused_plan if fits and rows % 128 == 0 and by_partials < by_weights else gathered_plan
    return plan(
        grad_out, out_weight, row_owner, row_position, query_rows, key_rows, value_rows, band_widths
    )


def solution(mesh):
    return jax.shard_map(
        per_device,
        mesh=mesh,
        in_specs=(
            P("seq", "head"),
            P("head", "seq"),
            P("seq"),
            P("seq"),
            P("seq", "head"),
            P("seq", "head"),
            P("seq", "head"),
            P("seq", None),
        ),
        out_specs=(P("seq", "head"), P("seq", "head"), P("seq", "head")),
        check_vma=False,
    )
```

```python
import functools

import jax
import jax.numpy as jnp
from jax import lax
from jax.experimental import pallas as pl
from jax.experimental.pallas import tpu as pltpu
from jax.sharding import PartitionSpec as P

HEAD_DIM = 128


DISTANCES = (0, 1, 2, 4)
NEG_FILL = -1e30


def shifted(value, axis, by):
    peers = lax.axis_size(axis)
    pairs = [(i, i + by) for i in range(peers) if 0 <= i + by < peers]
    return lax.ppermute(value, axis, pairs)


def gathered_plan(
    grad_out, out_weight, row_owner, row_position, query_rows, key_rows, value_rows, band_widths
):
    frame_len = query_rows.shape[0]
    width = query_rows.shape[1]
    heads = width // HEAD_DIM
    scale = HEAD_DIM ** (-0.5)
    full_grad = lax.all_gather(grad_out, "head", axis=1, tiled=True)
    packed = jnp.einsum(
        "rc,hc->rh",
        full_grad,
        lax.all_gather(out_weight, "seq", axis=1, tiled=True),
        preferred_element_type=jnp.float32,
    ).astype(jnp.bfloat16)
    owners = lax.axis_size("seq")
    capacity = max(1, 3 * frame_len // (2 * owners))
    order_ids = jnp.arange(frame_len)
    same_owner = (row_owner[:, None] == row_owner[None, :]) & (
        order_ids[None, :] < order_ids[:, None]
    )
    earlier = jnp.sum(same_owner.astype(jnp.int32), axis=1)
    slot_ids = row_owner * capacity + earlier
    placing = jnp.arange(owners * capacity)[:, None] == slot_ids[None, :]
    outgoing = jnp.dot(placing.astype(jnp.bfloat16), packed, preferred_element_type=jnp.float32)
    outgoing = outgoing.astype(jnp.bfloat16).reshape(owners, capacity, width)
    slot_pos = (
        jnp.dot(
            placing.astype(jnp.float32),
            (row_position + 1).astype(jnp.float32),
            precision=lax.Precision.HIGHEST,
        )
        - 1.0
    )
    slot_pos = slot_pos.reshape(owners, capacity).astype(jnp.bfloat16)
    incoming, incoming_pos = (
        lax.all_to_all(outgoing, "seq", split_axis=0, concat_axis=0, tiled=True),
        lax.all_to_all(slot_pos, "seq", split_axis=0, concat_axis=0, tiled=True),
    )
    landing = (
        incoming_pos.reshape(-1).astype(jnp.float32)[None, :]
        == jnp.arange(frame_len, dtype=jnp.float32)[:, None]
    )
    grad_attn = jnp.dot(
        landing.astype(jnp.bfloat16),
        incoming.reshape(-1, width),
        preferred_element_type=jnp.float32,
    ).astype(jnp.bfloat16)
    frame = lax.axis_index("seq")
    remote = {}
    for distance in (1, 2, 4):
        remote[distance] = shifted((key_rows, value_rows), "seq", distance)
    remote[0] = (key_rows, value_rows)
    positions = jnp.arange(frame_len)
    spread = jnp.abs(positions[:, None] - positions[None, :])
    limits = {0: frame_len, 1: frame_len, 2: band_widths[0, 0], 4: band_widths[0, 1]}
    mask_list = [(frame - distance >= 0) & (spread < limits[distance]) for distance in DISTANCES]
    usable = jnp.concatenate(mask_list, axis=1)[None]
    key_all = jnp.concatenate([remote[distance][0] for distance in DISTANCES], axis=0)
    value_all = jnp.concatenate([remote[distance][1] for distance in DISTANCES], axis=0)
    key_heads = key_all.reshape(4 * frame_len, heads, HEAD_DIM)
    value_heads = value_all.reshape(4 * frame_len, heads, HEAD_DIM)
    query_heads = query_rows.reshape(frame_len, heads, HEAD_DIM)
    grad_heads = grad_attn.reshape(frame_len, heads, HEAD_DIM)
    scores = (
        jnp.einsum("ihc,jhc->hij", query_heads, key_heads, preferred_element_type=jnp.float32)
        * scale
    )
    row_max = jnp.max(jnp.where(usable, scores, NEG_FILL), axis=2, keepdims=True)
    weights = jnp.where(usable, jnp.exp(scores - row_max), 0.0)
    row_sum = jnp.sum(weights, axis=2, keepdims=True)
    attn_prob = weights / row_sum
    prob_half = attn_prob.astype(jnp.bfloat16)
    attn_out = jnp.einsum(
        "hij,jhc->ihc", prob_half, value_heads, preferred_element_type=jnp.float32
    )
    row_dot = jnp.sum(grad_heads.astype(jnp.float32) * attn_out, axis=2).T[:, :, None]
    grad_prob = jnp.einsum(
        "ihc,jhc->hij", grad_heads, value_heads, preferred_element_type=jnp.float32
    )
    grad_score = (attn_prob * (grad_prob - row_dot)).astype(jnp.bfloat16)
    grad_query = scale * jnp.einsum(
        "hij,jhc->ihc", grad_score, key_heads, preferred_element_type=jnp.float32
    )
    grad_query = grad_query.reshape(frame_len, width).astype(jnp.bfloat16)
    local_score = grad_score[:, :, :frame_len]
    local_half = prob_half[:, :, :frame_len]
    key_sum = scale * jnp.einsum(
        "hij,ihc->jhc", local_score, query_heads, preferred_element_type=jnp.float32
    )
    value_sum = jnp.einsum(
        "hij,ihc->jhc", local_half, grad_heads, preferred_element_type=jnp.float32
    )
    log_norm = (row_max + jnp.log(row_sum))[:, :, 0]
    stats_local = (log_norm, row_dot[:, :, 0], band_widths.astype(jnp.float32))
    own_keys = key_rows.reshape(frame_len, heads, HEAD_DIM)
    own_values = value_rows.reshape(frame_len, heads, HEAD_DIM)
    for distance in (1, 2, 4):
        query_recv, grad_recv = shifted((query_rows, grad_attn), "seq", -distance)
        norm_recv, dot_recv, band_recv = shifted(
            (stats_local[0], stats_local[1], stats_local[2]), "seq", -distance
        )
        if distance == 2:
            limit = band_recv[0, 0]
        elif distance == 4:
            limit = band_recv[0, 1]
        else:
            limit = jnp.float32(frame_len)
        valid = ((frame + distance < owners) & (spread.astype(jnp.float32) < limit))[None]
        query_far = query_recv.reshape(frame_len, heads, HEAD_DIM)
        grad_far = grad_recv.reshape(frame_len, heads, HEAD_DIM)
        far_scores = (
            jnp.einsum("ihc,jhc->hij", query_far, own_keys, preferred_element_type=jnp.float32)
            * scale
        )
        far_prob = jnp.where(valid, jnp.exp(far_scores - norm_recv[:, :, None]), 0.0)
        far_grad_prob = jnp.einsum(
            "ihc,jhc->hij", grad_far, own_values, preferred_element_type=jnp.float32
        )
        far_score = (far_prob * (far_grad_prob - dot_recv[:, :, None])).astype(jnp.bfloat16)
        key_sum = key_sum + scale * jnp.einsum(
            "hij,ihc->jhc", far_score, query_far, preferred_element_type=jnp.float32
        )
        value_sum = value_sum + jnp.einsum(
            "hij,ihc->jhc",
            far_prob.astype(jnp.bfloat16),
            grad_far,
            preferred_element_type=jnp.float32,
        )
    key_sum = key_sum.reshape(frame_len, width)
    value_sum = value_sum.reshape(frame_len, width)
    return (grad_query, key_sum.astype(jnp.bfloat16), value_sum.astype(jnp.bfloat16))


def dot(a, b, contract):
    return lax.dot_general(a, b, (contract, ((), ())), preferred_element_type=jnp.float32)


def fused_kernel(
    owners, groups,
    go_in, w_in, info, q_in, k_in, v_in, band,
    dq_out, dk_out, dv_out,
    go, wpair, q, k, v, rsend, grows, codes, tall, zsend, zrecv, kv, prob, half, attn, grad, score,
    part, back, total, send_sem, recv_sem, load_sem,
):
    frame_len, width = q.shape
    depth = w_in.shape[1]
    cap = rsend.shape[1]
    heads = width // HEAD_DIM
    ratio = owners // groups
    shares = owners // groups
    pairs = owners // 2
    scale = HEAD_DIM ** (-0.5)
    s = lax.axis_index("seq")
    g = lax.axis_index("head")
    odd = lax.rem(s, 2)
    even = odd == 0
    peer = s + 1 - 2 * odd
    level = s // 2
    used = [0]
    pending = []

    def copy(src, dst, sem, ds, dg):
        used[0] += 1
        return pltpu.make_async_remote_copy(
            src_ref=src, dst_ref=dst, send_sem=send_sem.at[used[0] - 1], recv_sem=recv_sem.at[sem],
            device_id={"seq": ds, "head": dg}, device_id_type=pl.DeviceIdType.MESH,
        )

    def when(cond, action):
        if cond is None:
            action()
        else:
            pl.when(cond)(action)

    def send(cond, src, dst, sem, ds, dg):
        moving = copy(src, dst, sem, ds, dg)
        when(cond, lambda: moving.start())
        pending.append((cond, moving))

    def arrive(cond, dst, sem, ds, dg):
        moving = pltpu.make_async_remote_copy(
            src_ref=dst, dst_ref=dst, send_sem=send_sem.at[0], recv_sem=recv_sem.at[sem],
            device_id={"seq": ds, "head": dg}, device_id_type=pl.DeviceIdType.MESH,
        )
        when(cond, lambda: moving.wait_recv())

    sem_rows = 0
    sem_tgt = owners
    sem_w = 2 * owners
    sem_z = sem_w + 1
    sem_kv = sem_z + pairs
    sem_back = sem_kv + 6

    relay = lax.rem(s, groups)
    source_group = s // ratio
    alone = (source_group == g) & (relay == g)

    barrier = pltpu.get_barrier_semaphore()

    def greet(ds, dg):
        pl.semaphore_signal(
            barrier, inc=1, device_id={"seq": ds, "head": dg}, device_id_type=pl.DeviceIdType.MESH
        )

    for i in range(1, owners):
        greet(lax.rem(s + i, owners), g)
    for i in range(1, groups):
        greet(s, lax.rem(g + i, groups))
    for i in range(ratio):
        ds = ratio * g + i
        pl.when((ds != s) | (relay != g))(functools.partial(greet, ds, relay))
    for i in range(shares):
        origin = g + i * groups
        pl.when((origin != s) | (source_group != g))(functools.partial(greet, origin, source_group))
    loads = [
        pltpu.make_async_copy(src, dst, load_sem.at[i])
        for i, (src, dst) in enumerate(
            ((go_in, go), (k_in, k), (v_in, v), (q_in, q), (w_in, wpair.at[odd]))
        )
    ]
    for moving in loads:
        moving.start()

    row_ids = lax.broadcasted_iota(jnp.int32, (frame_len, frame_len), 0)
    col_ids = lax.broadcasted_iota(jnp.int32, (frame_len, frame_len), 1)
    earlier = jnp.where(row_ids < col_ids, 1.0, 0.0).astype(jnp.bfloat16)
    chosen = []
    for parity in range(2):
        member = jnp.where(info[2] == parity, 1.0, 0.0)
        rank = dot(member.astype(jnp.bfloat16), earlier, ((1,), (0,)))
        slot = jnp.where(member > 0.5, rank, -1.0)[0:1]
        choose = jnp.where(row_ids.astype(jnp.float32) == slot, 1.0, 0.0).astype(jnp.bfloat16)
        owner = dot(info[0].astype(jnp.bfloat16), choose, ((1,), (1,)))
        place = dot(info[1].astype(jnp.bfloat16), choose, ((1,), (1,)))
        codes[parity] = (owner - 1.0) * frame_len + place
        chosen.append(choose[:cap])
    loads[0].wait()
    for parity in range(2):
        rsend[parity] = dot(chosen[parity], go[...], ((1,), (0,))).astype(jnp.bfloat16)

    greetings = owners - 1 + groups - 1 + ratio + shares
    pl.semaphore_wait(barrier, jnp.where(alone, greetings - 2, greetings))

    for i in range(ratio):
        ds = ratio * g + i
        own = (ds == s) & (relay == g)

        def keep(i=i):
            grows[s] = rsend[i]

        pl.when(own)(keep)
        send(jnp.logical_not(own), rsend.at[i], grows.at[s], sem_rows + s, ds, relay)
    tall[s] = codes[odd]
    for i in range(1, owners):
        ds = lax.rem(s + i, owners)
        send(None, codes.at[lax.rem(ds, 2)], tall.at[s], sem_tgt + s, ds, g)
    send(None, w_in, wpair.at[odd], sem_w, peer, g)

    has_two = s + 2 < owners
    for j, ref in enumerate((k_in, v_in)):
        send(has_two, ref, kv.at[1, j], sem_kv + 2 + j, jnp.minimum(s + 2, owners - 1), g)
    for j, ref in enumerate((k_in, v_in)):
        send(even, ref, kv.at[0, j], sem_kv + j, peer, g)

    def clear(slot):
        kv[slot] = jnp.zeros((2, frame_len, width), jnp.bfloat16)

    pl.when(s < 1)(lambda: clear(0))
    pl.when(s < 2)(lambda: clear(1))
    pl.when(s < 4)(lambda: clear(2))

    for i in range(shares):
        origin = g + i * groups
        own = (origin == s) & (source_group == g)
        arrive(jnp.logical_not(own), grows.at[origin], sem_rows + origin, origin, source_group)
        for j in range(1, groups):
            send(None, grows.at[origin], grows.at[origin], sem_rows + origin, s, lax.rem(g + j, groups))
    for j in range(1, groups):
        via = lax.rem(g + j, groups)
        for i in range(shares):
            origin = via + i * groups
            arrive(None, grows.at[origin], sem_rows + origin, s, via)
    for i in range(1, owners):
        origin = lax.rem(s + i, owners)
        arrive(None, tall.at[origin], sem_tgt + origin, origin, g)

    has_back = s >= 2
    behind = jnp.maximum(s - 2, 0)
    ahead = jnp.minimum(s + 2, owners - 1)
    for j in range(2):
        arrive(has_back, kv.at[1, j], sem_kv + 2 + j, behind, g)
        send(has_back & has_two, kv.at[1, j], kv.at[2, j], sem_kv + 4 + j, ahead, g)
        send(has_back & (odd == 1), kv.at[1, j], kv.at[0, j], sem_kv + j, peer, g)

    for moving in loads[1:]:
        moving.wait()
    arrive(None, wpair.at[1 - odd], sem_w, peer, g)
    code = jnp.concatenate([tall[o][:, :cap] for o in range(owners)], axis=1)[0:1]
    lane_rows = lax.broadcasted_iota(jnp.int32, (frame_len, owners * cap), 0)
    pick = jnp.concatenate(
        [
            jnp.where(
                code == (lane_rows + (2 * z + odd) * frame_len).astype(jnp.float32), 1.0, 0.0
            ).astype(jnp.bfloat16)
            for z in range(pairs)
        ],
        axis=0,
    )
    rows = dot(pick, grows[...].reshape(owners * cap, width), ((1,), (0,))).astype(jnp.bfloat16)
    sums = dot(rows[:, :depth], wpair[0], ((1,), (1,))) + dot(rows[:, depth:], wpair[1], ((1,), (1,)))
    zsend[...] = sums.astype(jnp.bfloat16).reshape(pairs, frame_len, width)
    for i in range(1, pairs):
        z = lax.rem(level + i, pairs)
        send(None, zsend.at[z], zrecv.at[level], sem_z + level, 2 * z + odd, g)
    zrecv[level] = zsend[level]

    has_one = s >= 1
    has_four = s >= 4
    for j in range(2):
        arrive(has_one, kv.at[0, j], sem_kv + j, peer, g)
    for j in range(2):
        arrive(has_four, kv.at[2, j], sem_kv + 4 + j, behind, g)
    spread = jnp.abs(row_ids - col_ids)
    limits = (
        frame_len,
        jnp.where(s >= 1, frame_len, 0),
        jnp.where(s >= 2, band[0, 0], 0),
        jnp.where(s >= 4, band[0, 1], 0),
    )
    masks = [spread < limit for limit in limits]

    def lanes(h):
        return slice(h * HEAD_DIM, (h + 1) * HEAD_DIM)

    def tokens(d):
        return slice(d * frame_len, (d + 1) * frame_len)

    def far_heads(j, ref, h):
        return [ref[:, lanes(h)]] + [kv[d, j, :, lanes(h)] for d in range(3)]

    for h in range(heads):
        qh = q[:, lanes(h)]
        keys = jnp.concatenate(far_heads(0, k, h), axis=0)
        values = jnp.concatenate(far_heads(1, v, h), axis=0)
        usable = jnp.concatenate([jnp.where(m, 1.0, 0.0) for m in masks], axis=1) > 0.5
        scores = dot(qh, keys, ((1,), (1,))) * scale
        row_max = jnp.max(jnp.where(usable, scores, NEG_FILL), axis=1, keepdims=True)
        weights = jnp.where(usable, jnp.exp(scores - row_max), 0.0)
        probs = weights / jnp.sum(weights, axis=1, keepdims=True)
        prob[h] = probs
        half[h] = probs.astype(jnp.bfloat16)
        attn[h] = dot(probs.astype(jnp.bfloat16), values, ((1,), (0,)))

    for i in range(1, pairs):
        z = lax.rem(level + i, pairs)
        arrive(None, zrecv.at[z], sem_z + z, 2 * z + odd, g)
    grad[...] = sum(zrecv[z].astype(jnp.float32) for z in range(pairs)).astype(jnp.bfloat16)

    for h in range(heads):
        gh = grad[:, lanes(h)]
        values = jnp.concatenate(far_heads(1, v, h), axis=0)
        row_dot = jnp.sum(gh.astype(jnp.float32) * attn[h], axis=1, keepdims=True)
        grad_prob = dot(gh, values, ((1,), (1,)))
        score[h] = (prob[h] * (grad_prob - row_dot)).astype(jnp.bfloat16)

    def key_part(h, d):
        return dot(score[h, :, tokens(d)], q[:, lanes(h)], ((0,), (0,)))

    def value_part(h, d):
        return dot(half[h, :, tokens(d)], grad[:, lanes(h)], ((0,), (0,)))

    for h in range(heads):
        part[0, 0, :, lanes(h)] = key_part(h, 3).astype(jnp.bfloat16)
        part[0, 1, :, lanes(h)] = value_part(h, 3).astype(jnp.bfloat16)
    for j in range(2):
        send(has_four, part.at[0, j], back.at[0, j], sem_back + j, behind, g)
    for h in range(heads):
        part[1, 0, :, lanes(h)] = key_part(h, 1).astype(jnp.bfloat16)
        part[1, 1, :, lanes(h)] = value_part(h, 1).astype(jnp.bfloat16)
    for j in range(2):
        send(has_one, part.at[1, j], back.at[1, j], sem_back + 2 + j, peer, g)
    for h in range(heads):
        total[0, :, lanes(h)] = key_part(h, 2)
        total[1, :, lanes(h)] = value_part(h, 2)

    def add(slot, j):
        total[j] += back[slot, j].astype(jnp.float32)

    passed = has_back & has_two
    for j in range(2):
        arrive((odd == 0) | (s >= 3), back.at[1, j], sem_back + 2 + j, peer, g)
        pl.when((odd == 1) & (s >= 3))(functools.partial(add, 1, j))
        arrive(passed, back.at[0, j], sem_back + j, ahead, g)
        pl.when(passed)(functools.partial(add, 0, j))
        part[2, j] = total[j].astype(jnp.bfloat16)
        send(has_back, part.at[2, j], back.at[2, j], sem_back + 4 + j, behind, g)

    for h in range(heads):
        total[0, :, lanes(h)] = key_part(h, 0)
        total[1, :, lanes(h)] = value_part(h, 0)
        keys = jnp.concatenate(far_heads(0, k, h), axis=0)
        dq_out[:, lanes(h)] = (scale * dot(score[h], keys, ((1,), (0,)))).astype(jnp.bfloat16)
    for j, out in enumerate((dk_out, dv_out)):
        pl.when(even)(functools.partial(add, 1, j))
        arrive(has_two, back.at[2, j], sem_back + 4 + j, ahead, g)
        pl.when(has_two)(functools.partial(add, 2, j))
        out[...] = ((scale if j == 0 else 1.0) * total[j]).astype(jnp.bfloat16)
    for cond, moving in pending:
        when(cond, lambda moving=moving: moving.wait_send())


def fused_plan(
    grad_out, out_weight, row_owner, row_position, query_rows, key_rows, value_rows, band_widths
):
    owners = lax.axis_size("seq")
    groups = lax.axis_size("head")
    frame_len, width = query_rows.shape
    depth = out_weight.shape[1]
    heads = width // HEAD_DIM
    pairs = owners // 2
    cap = pairs * max(1, 3 * frame_len // (2 * owners))
    cap = min(frame_len, -(-cap // 16) * 16)
    info = jnp.stack([row_owner + 1, row_position, row_owner % 2]).astype(jnp.float32)
    info = jnp.broadcast_to(info[:, None, :], (3, 8, frame_len))
    half = jnp.bfloat16
    vmem = pl.BlockSpec(memory_space=pltpu.VMEM)
    hbm = pl.BlockSpec(memory_space=pltpu.HBM)
    out = jax.ShapeDtypeStruct((frame_len, width), half)
    return pl.pallas_call(
        functools.partial(fused_kernel, owners, groups),
        out_shape=(out, out, out),
        in_specs=[hbm, hbm, vmem, hbm, hbm, hbm, pl.BlockSpec(memory_space=pltpu.SMEM)],
        out_specs=(vmem, vmem, vmem),
        scratch_shapes=[
            pltpu.VMEM((frame_len, width), half),
            pltpu.VMEM((2, width, depth), half),
            pltpu.VMEM((frame_len, width), half),
            pltpu.VMEM((frame_len, width), half),
            pltpu.VMEM((frame_len, width), half),
            pltpu.VMEM((2, cap, width), half),
            pltpu.VMEM((owners, cap, width), half),
            pltpu.VMEM((2, 8, frame_len), jnp.float32),
            pltpu.VMEM((owners, 8, frame_len), jnp.float32),
            pltpu.VMEM((pairs, frame_len, width), half),
            pltpu.VMEM((pairs, frame_len, width), half),
            pltpu.VMEM((3, 2, frame_len, width), half),
            pltpu.VMEM((heads, frame_len, 4 * frame_len), jnp.float32),
            pltpu.VMEM((heads, frame_len, 4 * frame_len), half),
            pltpu.VMEM((heads, frame_len, HEAD_DIM), jnp.float32),
            pltpu.VMEM((frame_len, width), half),
            pltpu.VMEM((heads, frame_len, 4 * frame_len), half),
            pltpu.VMEM((3, 2, frame_len, width), half),
            pltpu.VMEM((3, 2, frame_len, width), half),
            pltpu.VMEM((2, frame_len, width), jnp.float32),
            pltpu.SemaphoreType.DMA((96,)),
            pltpu.SemaphoreType.DMA((3 * owners + 13,)),
            pltpu.SemaphoreType.DMA((5,)),
        ],
        compiler_params=pltpu.CompilerParams(
            collective_id=0, has_side_effects=True, vmem_limit_bytes=62 * 1024 * 1024
        ),
    )(grad_out, out_weight, info, query_rows, key_rows, value_rows, band_widths)


def per_device(
    grad_out, out_weight, row_owner, row_position, query_rows, key_rows, value_rows, band_widths
):
    owners = lax.axis_size("seq")
    groups = lax.axis_size("head")
    rows, width = query_rows.shape
    depth = out_weight.shape[1]
    model = owners * depth
    by_partials = owners * rows * width
    by_weights = model * (width + rows)
    fits = owners == 2 * groups and owners >= 4 and depth % 128 == 0
    plan = fused_plan if fits and rows % 128 == 0 and by_partials < by_weights else gathered_plan
    return plan(
        grad_out, out_weight, row_owner, row_position, query_rows, key_rows, value_rows, band_widths
    )


def solution(mesh):
    return jax.shard_map(
        per_device,
        mesh=mesh,
        in_specs=(
            P("seq", "head"),
            P("head", "seq"),
            P("seq"),
            P("seq"),
            P("seq", "head"),
            P("seq", "head"),
            P("seq", "head"),
            P("seq", None),
        ),
        out_specs=(P("seq", "head"), P("seq", "head"), P("seq", "head")),
        check_vma=False,
    )
```
